512 devices in a mesh: row: 32 (over z, x_lo), col: 16 (over x_hi, y, core).
Axes of the slice: x: 4 (x_hi: 2, x_lo: 2; x = x_hi * 2 + x_lo), y: 4, z: 16, core: 2. Of those that a mesh axis runs over, the one named last changes fastest.
Arguments:
- amplitudes: bfloat16 [2048, 16384], P('col', 'row'), may hold values from -6 to 6
- integrals: bfloat16 [2048, 16384], P('row', 'col'), may hold values from -0.125 to 0.125
- tile_mask: int32 [16, 128], P('col', 'row'), may hold values from 0 to 1, as said below
Outputs:
- residual: bfloat16 [16384, 16384], P('row', 'col')
The draws below stay inside these ranges and needn't reach their ends.
Inputs may be any that keep to these rules, and one draw needn't show every extreme that they name: tile_mask is 0 or 1 for each tile.
All inputs are finite; a program needn't handle non-finite values.
Results may differ from the reference program's by a relative error of at most 0.001.
Values may be sent and summed in bfloat16 or wider, within the bound.
No kernel may reach another device: no remote copies, remote signals or barrier semaphores. Data moves between devices by JAX's collectives and lax.ppermute only.
A program may use at most 64 MiB of HBM per device.

```python
import jax
import jax.numpy as jnp
from jax import lax

OCC = 128
PAIRS = 16384
KTILE = 128
PTILE = 128
KV = 2048
NAB = 16384


def draw_tile_mask(key, part):
    key = jax.random.fold_in(key, 7)
    tile_rows = KV // KTILE
    pair_tiles = OCC * OCC // PTILE
    virt_index = jnp.arange(tile_rows, dtype=jnp.int32)[:, None]
    pair_index = jnp.arange(pair_tiles, dtype=jnp.int32)[None, :]
    occ_index = pair_index * PTILE // OCC
    centre = occ_index * tile_rows // OCC
    band_width = jnp.where(occ_index < OCC // 4, tile_rows, 1)
    close_band = jnp.abs(virt_index - centre) <= band_width
    key_keep, key_stray = jax.random.split(key)
    kept_tile = jax.random.randint(key_keep, (tile_rows, pair_tiles), 0, 4) > 0
    stray_tile = jax.random.randint(key_stray, (tile_rows, pair_tiles), 0, 16) == 0
    return (close_band & kept_tile | stray_tile).astype(jnp.int32)


def block_scale(key, shape, shards, smallest, high):
    level = 1.0
    for dim, parts in shards:
        steps = jax.random.uniform(jax.random.fold_in(jax.random.fold_in(key, 6), dim), (parts,), jnp.float32, smallest / len(shards), high / len(shards))
        level = level * jnp.repeat(jnp.exp(steps), shape[dim] // parts).reshape((-1,) + (1,) * (len(shape) - 1 - dim))
    return level


def normal_values(rng, shape, deviation, reach, cuts=(), held_as=jnp.bfloat16):
    factor_of = block_scale(rng, shape, cuts, -0.22, 0.18) if cuts else 1.0
    result = jax.random.normal(rng, shape, jnp.float32) * deviation * factor_of
    return jnp.minimum(jnp.maximum(result, -reach), reach).astype(held_as)


def setup_inputs(seed: int = 0) -> dict:
    splits = jax.random.split(jax.random.key(seed), 4)
    amplitudes = normal_values(splits[0], (KV, PAIRS), 1.0, 6.0, ((0, 16), (1, 32)))
    integrals = normal_values(splits[1], (KV, NAB), KV ** -0.5, 0.125, ((0, 32), (1, 16)))
    tile_mask = draw_tile_mask(jax.random.fold_in(splits[3], 71), 0)
    return dict(amplitudes=amplitudes, integrals=integrals, tile_mask=tile_mask)


def reference(amplitudes, integrals, tile_mask):
    tile_rows, tile_cols = tile_mask.shape
    blocks = amplitudes.reshape(tile_rows, KTILE, tile_cols, PTILE)
    blocks = blocks * tile_mask.astype(jnp.bfloat16)[:, None, :, None]
    masked = blocks.reshape(KV, PAIRS)
    ladder = lax.dot_general(masked, integrals, (((0,), (0,)), ((), ())), preferred_element_type=jnp.float32)
    square = ladder.reshape(OCC, OCC, NAB)
    return (square - square.transpose(1, 0, 2)).reshape(PAIRS, NAB).astype(jnp.bfloat16)
```

```python
import jax
import jax.numpy as jnp
from jax import lax
from jax.sharding import PartitionSpec as P

OI = 4
ZN = 16


def mask_tiles(amplitudes, tile_mask):
    virt_rows, pair_count = amplitudes.shape
    tile_rows, tile_cols = tile_mask.shape
    blocks = amplitudes.reshape(
        tile_rows, virt_rows // tile_rows, tile_cols, pair_count // tile_cols
    )
    scaled = blocks * tile_mask.astype(jnp.bfloat16)[:, None, :, None]
    return scaled.reshape(virt_rows, pair_count)


def product(left, right):
    return lax.dot_general(
        left, right, (((0,), (0,)), ((), ())), preferred_element_type=jnp.float32
    )


def z_shift(x, d):
    return lax.ppermute(x, "row", [(r, (r + 2 * d) % 32) for r in range(32)])


def x_swap(x):
    return lax.ppermute(x, "row", [(r, r ^ 1) for r in range(32)])


def core_swap(x):
    return lax.ppermute(x, "col", [(c, c ^ 1) for c in range(16)])


CORE_GROUPS = [list(range(c, 16, 2)) for c in range(2)]


def gather_half(x):
    return lax.all_gather(x, "col", axis=0, tiled=True, axis_index_groups=CORE_GROUPS)


def put(whole, block, *starts):
    zero = jnp.int32(0)
    starts = starts + (zero,) * (whole.ndim - len(starts))
    return lax.dynamic_update_slice(whole, block, starts)


def on_device(amplitudes, integrals, tile_mask):
    row_count = lax.axis_size("row")
    row = lax.axis_index("row")
    core = lax.axis_index("col") % 2
    z = row // 2
    xl = row % 2
    rows, cols = integrals.shape

    masked = mask_tiles(amplitudes, tile_mask)
    arranged = masked.reshape(masked.shape[0], OI, row_count, OI).transpose(0, 3, 2, 1)

    up4 = z_shift(integrals, 4)
    down4 = z_shift(integrals, -4)
    far = z_shift(integrals, 8)

    swapped = lax.all_to_all(arranged, "row", split_axis=2, concat_axis=2, tiled=True).reshape(
        masked.shape
    )
    own_half = gather_half(masked)
    swap_half = gather_half(swapped)
    own_other = core_swap(own_half)
    swap_other = core_swap(swap_half)

    q = z // 4
    block = jnp.zeros((4, rows, cols), integrals.dtype)
    block = put(block, integrals[None], q)
    block = put(block, up4[None], (q + 3) % 4)
    block = put(block, down4[None], (q + 1) % 4)
    block = put(block, far[None], (q + 2) % 4)

    partner = x_swap(block)
    two = z_shift(block, 2)
    two_partner = x_swap(two)
    up = z_shift(block, 1)
    down = z_shift(block, -1)
    up_partner = z_shift(partner, 1)
    down_partner = z_shift(partner, -1)

    whole = jnp.zeros((2, 4, 2, 2, rows, cols), integrals.dtype)
    for got, got_partner, shift in (
        (block, partner, 0),
        (two, two_partner, 2),
        (up, up_partner, 3),
        (down, down_partner, 1),
    ):
        m = (z + shift) % 4
        side = (m % 2 + core) % 2
        for part, x_index in ((got, xl), (got_partner, 1 - xl)):
            whole = put(whole, part[None, :, None, None], side, jnp.int32(0), m // 2, x_index)
    same = whole[0].reshape(-1, cols)
    other = whole[1].reshape(-1, cols)
    difference = (
        product(own_half, same)
        - product(swap_half, same)
        + product(own_other, other)
        - product(swap_other, other)
    )
    return difference.astype(jnp.bfloat16)


def solution(mesh):
    in_specs = (P("col", "row"), P("row", "col"), P("col", "row"))
    out_specs = P("row", "col")
    return jax.shard_map(
        on_device, mesh=mesh, in_specs=in_specs, out_specs=out_specs, check_vma=False
    )
```

```python
import jax
import jax.numpy as jnp
from jax import lax
from jax.sharding import PartitionSpec as P

OI = 4
CORE_GROUPS = [list(range(c, 16, 2)) for c in range(2)]


def z_shift(x, d):
    return lax.ppermute(x, "row", [(r, (r + 2 * d) % 32) for r in range(32)])


def x_swap(x):
    return lax.ppermute(x, "row", [(r, r ^ 1) for r in range(32)])


def core_swap(x):
    return lax.ppermute(x, "col", [(c, c ^ 1) for c in range(16)])


def put(whole, block, *starts):
    starts = tuple(jnp.int32(s) for s in starts)
    starts = starts + (jnp.int32(0),) * (whole.ndim - len(starts))
    return lax.dynamic_update_slice(whole, block, starts)


def product(left, right):
    return lax.dot_general(
        left, right, (((0, 2), (0, 1)), ((), ())), preferred_element_type=jnp.float32
    )


def on_device(amplitudes, integrals, tile_mask):
    row = lax.axis_index("row")
    core = lax.axis_index("col") % 2
    z = row // 2
    xl = row % 2
    rows, cols = integrals.shape
    depth, pairs = amplitudes.shape

    far = z_shift(integrals, 8)
    up4 = z_shift(integrals, 4)
    down4 = z_shift(integrals, -4)

    scale = jnp.repeat(tile_mask.astype(jnp.bfloat16).reshape(-1), pairs // OI)
    masked = (amplitudes * scale[None, :]).T
    sent = masked.reshape(OI, 32, OI, depth).transpose(1, 2, 0, 3)
    got = lax.all_to_all(sent, "row", split_axis=0, concat_axis=0, tiled=True)
    swapped = got.transpose(1, 0, 2, 3).reshape(pairs, depth)

    both = jnp.stack([masked, swapped])
    copies = jnp.broadcast_to(both[None], (8,) + both.shape)
    own = lax.all_to_all(
        copies, "col", split_axis=0, concat_axis=0, tiled=True, axis_index_groups=CORE_GROUPS
    )
    other = core_swap(own)

    block = jnp.stack([integrals, up4, down4, far])
    two = z_shift(block, 2)
    partner = x_swap(block)
    up = z_shift(block, 1)
    down = z_shift(block, -1)
    up_partner = z_shift(partner, 1)
    down_partner = z_shift(partner, -1)
    two_partner = x_swap(two)

    whole = jnp.zeros((2, 8, 2, rows, cols), integrals.dtype)
    for mine, theirs, shift in (
        (block, partner, 0),
        (two, two_partner, -2),
        (up, up_partner, -1),
        (down, down_partner, 1),
    ):
        for slot, offset in enumerate((0, -4, 4, 8)):
            zz = (z + shift + offset + 32) % 16
            for part, x_index in ((mine, xl), (theirs, 1 - xl)):
                whole = put(
                    whole, part[slot][None, None, None], (zz + core) % 2, zz // 2, x_index
                )
    same = whole[0].reshape(8, -1, cols)
    across = whole[1].reshape(8, -1, cols)
    difference = (
        product(own[:, 0], same)
        - product(own[:, 1], same)
        + product(other[:, 0], across)
        - product(other[:, 1], across)
    )
    return difference.astype(jnp.bfloat16)


def solution(mesh):
    in_specs = (P("col", "row"), P("row", "col"), P("col", "row"))
    out_specs = P("row", "col")
    return jax.shard_map(
        on_device, mesh=mesh, in_specs=in_specs, out_specs=out_specs, check_vma=False
    )
```

```python
import jax
import jax.numpy as jnp
from jax import lax
from jax.experimental import pallas as pl
from jax.experimental.pallas import tpu as pltpu
from jax.sharding import PartitionSpec as P

OI = 4
CORE_GROUPS = [list(range(c, 16, 2)) for c in range(2)]
FAR_GROUPS = [[(4 * q + m) * 2 + x for q in range(4)] for m in range(4) for x in range(2)]
NTILE = 256


def z_shift(x, d):
    return lax.ppermute(x, "row", [(r, (r + 2 * d) % 32) for r in range(32)])


def x_swap(x):
    return lax.ppermute(x, "row", [(r, r ^ 1) for r in range(32)])


def core_swap(x):
    return lax.ppermute(x, "col", [(c, c ^ 1) for c in range(16)])


def spread(x, axis, groups):
    copies = jnp.broadcast_to(x[None], (len(groups[0]),) + x.shape)
    return lax.all_to_all(
        copies, axis, split_axis=0, concat_axis=0, tiled=True, axis_index_groups=groups
    )


def products(place, own, other, near, two, two_partner, up, down, out, ints, amps, sem):
    z, xl, core = place[0], place[1], place[2]
    copies = []
    for side, ref in enumerate((own, other)):
        for s in range(2):
            for g in range(8):
                copies.append((ref.at[g, s], amps.at[side, s, :, pl.ds(g * 128, 128)]))
    blocks = (
        (near.at[0], 0, xl),
        (near.at[1], 0, 1 - xl),
        (two, 2, xl),
        (two_partner, 2, 1 - xl),
        (up.at[0], 3, xl),
        (up.at[1], 3, 1 - xl),
        (down.at[0], 1, xl),
        (down.at[1], 1, 1 - xl),
    )
    for ref, shift, x_index in blocks:
        m = (z + shift) & 3
        copies.append((ref, ints.at[(m + core) & 1, :, m >> 1, x_index]))
    copies = [pltpu.make_async_copy(a, b, sem) for a, b in copies]
    for copy in copies:
        copy.start()
    for copy in copies:
        copy.wait()

    def tile(n, carry):
        cols = pl.ds(pl.multiple_of(n * NTILE, NTILE), NTILE)
        total = None
        for side in range(2):
            right = ints[side, :, :, :, :, cols].reshape(-1, NTILE)
            term = jnp.dot(
                amps[side, 0], right, preferred_element_type=jnp.float32
            ) - jnp.dot(amps[side, 1], right, preferred_element_type=jnp.float32)
            total = term if total is None else total + term
        out[:, cols] = total.astype(out.dtype)
        return carry

    lax.fori_loop(0, out.shape[1] // NTILE, tile, 0)


def on_device(amplitudes, integrals, tile_mask):
    row = lax.axis_index("row")
    place = jnp.stack([row // 2, row % 2, lax.axis_index("col") % 2]).astype(jnp.int32)
    rows, cols = integrals.shape
    depth, pairs = amplitudes.shape

    block = spread(integrals, "row", FAR_GROUPS)

    scale = jnp.repeat(tile_mask.astype(jnp.bfloat16).reshape(-1), pairs // OI)
    masked = (amplitudes * scale[None, :]).T
    sent = masked.reshape(OI, 32, OI, depth).transpose(1, 2, 0, 3)
    got = lax.all_to_all(sent, "row", split_axis=0, concat_axis=0, tiled=True)
    swapped = got.transpose(1, 0, 2, 3).reshape(pairs, depth)
    own = spread(jnp.stack([masked, swapped]), "col", CORE_GROUPS)
    other = core_swap(own)

    two = z_shift(block, 2)
    near = jnp.stack([block, x_swap(block)])
    up = z_shift(near, 1)
    down = z_shift(near, -1)
    two_partner = x_swap(two)

    anywhere = pl.BlockSpec(memory_space=pl.ANY)
    return pl.pallas_call(
        products,
        out_shape=jax.ShapeDtypeStruct((pairs, cols), jnp.bfloat16),
        in_specs=[pl.BlockSpec(memory_space=pltpu.SMEM)] + [anywhere] * 7,
        out_specs=pl.BlockSpec(memory_space=pltpu.VMEM),
        scratch_shapes=[
            pltpu.VMEM((2, 4, 2, 2, rows, cols), jnp.bfloat16),
            pltpu.VMEM((2, 2, pairs, 8 * depth), jnp.bfloat16),
            pltpu.SemaphoreType.DMA,
        ],
        compiler_params=pltpu.CompilerParams(vmem_limit_bytes=40 * 2**20),
        cost_estimate=pl.CostEstimate(
            flops=4 * pairs * 2048 * cols, bytes_accessed=9 * 2**20, transcendentals=0
        ),
    )(place, own, other, near, two, two_partner, up, down)


def solution(mesh):
    in_specs = (P("col", "row"), P("row", "col"), P("col", "row"))
    out_specs = P("row", "col")
    return jax.shard_map(
        on_device, mesh=mesh, in_specs=in_specs, out_specs=out_specs, check_vma=False
    )
```

```python
import jax
import jax.numpy as jnp
from jax import lax
from jax.experimental import pallas as pl
from jax.experimental.pallas import tpu as pltpu
from jax.sharding import PartitionSpec as P

OI = 4
CORE_GROUPS = [list(range(c, 16, 2)) for c in range(2)]
FAR = (0, -4, 4, 8)
NTILE = 256


def z_shift(x, d):
    return lax.ppermute(x, "row", [(r, (r + 2 * d) % 32) for r in range(32)])


def x_swap(x):
    return lax.ppermute(x, "row", [(r, r ^ 1) for r in range(32)])


def core_swap(x):
    return lax.ppermute(x, "col", [(c, c ^ 1) for c in range(16)])


def spread(x, axis, groups):
    copies = jnp.broadcast_to(x[None], (len(groups[0]),) + x.shape)
    return lax.all_to_all(
        copies, axis, split_axis=0, concat_axis=0, tiled=True, axis_index_groups=groups
    )


def products(place, own, other, near, two, two_partner, up, down, out, ints, amps, sem):
    z, xl, core = place[0], place[1], place[2]
    copies = []
    for side, ref in enumerate((own, other)):
        for s in range(2):
            for g in range(8):
                copies.append((ref.at[g, s], amps.at[side, s, :, pl.ds(g * 128, 128)]))
    blocks = (
        (near.at[0], 0, xl),
        (near.at[1], 0, 1 - xl),
        (two, -2, xl),
        (two_partner, -2, 1 - xl),
        (up.at[0], -1, xl),
        (up.at[1], -1, 1 - xl),
        (down.at[0], 1, xl),
        (down.at[1], 1, 1 - xl),
    )
    for ref, shift, x_index in blocks:
        for slot, offset in enumerate(FAR):
            k = (z + shift + offset) & 15
            copies.append((ref.at[slot], ints.at[(k + core) & 1, k >> 1, x_index]))
    copies = [pltpu.make_async_copy(a, b, sem) for a, b in copies]
    for copy in copies:
        copy.start()
    for copy in copies:
        copy.wait()

    def tile(n, carry):
        cols = pl.ds(pl.multiple_of(n * NTILE, NTILE), NTILE)
        total = None
        for side in range(2):
            right = ints[side, :, :, :, cols].reshape(-1, NTILE)
            term = jnp.dot(
                amps[side, 0], right, preferred_element_type=jnp.float32
            ) - jnp.dot(amps[side, 1], right, preferred_element_type=jnp.float32)
            total = term if total is None else total + term
        out[:, cols] = total.astype(out.dtype)
        return carry

    lax.fori_loop(0, out.shape[1] // NTILE, tile, 0)


def on_device(amplitudes, integrals, tile_mask):
    row = lax.axis_index("row")
    place = jnp.stack([row // 2, row % 2, lax.axis_index("col") % 2]).astype(jnp.int32)
    rows, cols = integrals.shape
    depth, pairs = amplitudes.shape

    far = z_shift(integrals, 8)
    up4 = z_shift(integrals, 4)
    down4 = z_shift(integrals, -4)
    block = jnp.stack([integrals, up4, down4, far])

    scale = jnp.repeat(tile_mask.astype(jnp.bfloat16).reshape(-1), pairs // OI)
    masked = (amplitudes * scale[None, :]).T
    sent = masked.reshape(OI, 32, OI, depth).transpose(1, 2, 0, 3)
    got = lax.all_to_all(sent, "row", split_axis=0, concat_axis=0, tiled=True)
    swapped = got.transpose(1, 0, 2, 3).reshape(pairs, depth)
    own = spread(jnp.stack([masked, swapped]), "col", CORE_GROUPS)
    other = core_swap(own)

    two = z_shift(block, 2)
    near = jnp.stack([block, x_swap(block)])
    up = z_shift(near, 1)
    down = z_shift(near, -1)
    two_partner = x_swap(two)

    anywhere = pl.BlockSpec(memory_space=pl.ANY)
    return pl.pallas_call(
        products,
        out_shape=jax.ShapeDtypeStruct((pairs, cols), jnp.bfloat16),
        in_specs=[pl.BlockSpec(memory_space=pltpu.SMEM)] + [anywhere] * 7,
        out_specs=pl.BlockSpec(memory_space=pltpu.VMEM),
        scratch_shapes=[
            pltpu.VMEM((2, 8, 2, rows, cols), jnp.bfloat16),
            pltpu.VMEM((2, 2, pairs, 8 * depth), jnp.bfloat16),
            pltpu.SemaphoreType.DMA,
        ],
        compiler_params=pltpu.CompilerParams(vmem_limit_bytes=40 * 2**20),
        cost_estimate=pl.CostEstimate(
            flops=4 * pairs * 2048 * cols, bytes_accessed=9 * 2**20, transcendentals=0
        ),
    )(place, own, other, near, two, two_partner, up, down)


def solution(mesh):
    in_specs = (P("col", "row"), P("row", "col"), P("col", "row"))
    out_specs = P("row", "col")
    return jax.shard_map(
        on_device, mesh=mesh, in_specs=in_specs, out_specs=out_specs, check_vma=False
    )
```

```python
import jax
import jax.numpy as jnp
from jax import lax
from jax.experimental import pallas as pl
from jax.experimental.pallas import tpu as pltpu
from jax.sharding import PartitionSpec as P

OI = 4
Q = 4
FAR_GROUPS = [[(4 * q + m) * 2 + x for q in range(4)] for m in range(4) for x in range(2)]
NEAR_GROUPS = [list(range(8 * q, 8 * q + 8)) for q in range(4)]
CORE_PAIRS = [[2 * g, 2 * g + 1] for g in range(8)]
STEPS = (((0, 1), (0, 3)), ((0, 2), (1, 0)), ((1, 1), (1, 3)), ((1, 2), (1, 2)))
NTILE = 256


def z_shift(x, d):
    return lax.ppermute(x, "row", [(r, (r + 2 * d) % 32) for r in range(32)])


def x_swap(x):
    return lax.ppermute(x, "row", [(r, r ^ 1) for r in range(32)])


def core_swap(x):
    return lax.ppermute(x, "col", [(c, c ^ 1) for c in range(16)])


def chip_shift(x, step):
    pairs = []
    for xh in range(2):
        for y in range(4):
            for c in range(2):
                dx, dy = step[c]
                pairs.append(((xh * 4 + y) * 2 + c, ((xh ^ dx) * 4 + (y + dy) % 4) * 2 + c))
    return lax.ppermute(x, "col", pairs)


def gather_chips(x):
    chip = lax.all_gather(x, "col", axis=0, axis_index_groups=CORE_PAIRS)
    got = [chip_shift(chip, step) for step in STEPS[:3]]
    got.append(chip_shift(x, STEPS[3])[None])
    return chip, jnp.concatenate(got)


def products(place, *refs):
    z, xl, core, xh, y = (place[i] for i in range(5))
    amp_refs, blocks, (out, ints, amps, sem) = refs[:6], refs[6:12], refs[12:]
    near_own, near_swap, two, two_partner, up, down = blocks
    copies = []

    def amp_copy(ref, s, dx, dy, c):
        col = ((xh ^ dx) * 4 + ((y - dy) & 3)) * 2 + c
        lanes = pl.ds(pl.multiple_of(col * 128, 128), 128)
        copies.append((ref, amps.at[s, :, lanes]))

    for s in range(2):
        chip, mine, theirs = amp_refs[3 * s : 3 * s + 3]
        for c in range(2):
            amp_copy(chip.at[c], s, 0, 0, c)
        for ref, who in ((mine, core), (theirs, 1 - core)):
            for n, step in enumerate(STEPS):
                dx = jnp.where(who == 0, step[0][0], step[1][0])
                dy = jnp.where(who == 0, step[0][1], step[1][1])
                if n < 3:
                    for c in range(2):
                        amp_copy(ref.at[2 * n + c], s, dx, dy, c)
                else:
                    amp_copy(ref.at[6], s, dx, dy, who)
    for ref, shift, x_index in (
        (near_own, 0, xl),
        (near_swap, 0, 1 - xl),
        (two, 2, xl),
        (two_partner, 2, 1 - xl),
        (up.at[0], 3, xl),
        (up.at[1], 3, 1 - xl),
        (down.at[0], 1, xl),
        (down.at[1], 1, 1 - xl),
    ):
        copies.append((ref, ints.at[:, (z + shift) & 3, x_index]))
    copies = [pltpu.make_async_copy(a, b, sem) for a, b in copies]
    for copy in copies:
        copy.start()
    for copy in copies:
        copy.wait()

    def tile(n, carry):
        cols = pl.ds(pl.multiple_of(n * NTILE, NTILE), NTILE)
        right = ints[:, :, :, :, cols].reshape(-1, NTILE)
        total = jnp.dot(amps[0], right, preferred_element_type=jnp.float32) - jnp.dot(
            amps[1], right, preferred_element_type=jnp.float32
        )
        out[:, cols] = total.astype(out.dtype)
        return carry

    lax.fori_loop(0, out.shape[1] // NTILE, tile, 0)


def on_device(amplitudes, integrals, tile_mask):
    row, col = lax.axis_index("row"), lax.axis_index("col")
    place = jnp.stack([row // 2, row % 2, col % 2, col // 8, col // 2 % 4]).astype(jnp.int32)
    rows, cols = integrals.shape
    depth, pairs = amplitudes.shape

    scale = jnp.repeat(tile_mask.astype(jnp.bfloat16).reshape(-1), pairs // OI)
    masked = (amplitudes * scale[None, :]).T

    sent = masked.reshape(OI, Q, 8, OI, depth).transpose(1, 2, 3, 0, 4).reshape(Q, -1, cols)
    load = jnp.concatenate([jnp.broadcast_to(integrals[None], (Q, rows, cols)), sent], axis=1)
    far = lax.all_to_all(
        load, "row", split_axis=0, concat_axis=0, tiled=True, axis_index_groups=FAR_GROUPS
    )
    amps = gather_chips(masked)
    block = far[:, :rows]
    hop, amps = lax.optimization_barrier((far[:, rows:], amps))
    hop = hop.reshape(Q, 8, OI, OI, depth).transpose(1, 0, 2, 3, 4)
    got = lax.all_to_all(
        hop, "row", split_axis=0, concat_axis=0, tiled=True, axis_index_groups=NEAR_GROUPS
    )
    swapped = got.transpose(2, 1, 0, 3, 4).reshape(pairs, depth)

    two = z_shift(block, 2)
    partner = x_swap(block)
    partner, two = lax.optimization_barrier((partner, two))
    near = jnp.stack([block, partner])
    up = z_shift(near, 1)
    down = z_shift(near, -1)
    two_partner = x_swap(two)
    swap_amps = gather_chips(swapped)

    anywhere = pl.BlockSpec(memory_space=pl.ANY)
    return pl.pallas_call(
        products,
        out_shape=jax.ShapeDtypeStruct((pairs, cols), jnp.bfloat16),
        in_specs=[pl.BlockSpec(memory_space=pltpu.SMEM)] + [anywhere] * 12,
        out_specs=pl.BlockSpec(memory_space=pltpu.VMEM),
        scratch_shapes=[
            pltpu.VMEM((Q, 4, 2, rows, cols), jnp.bfloat16),
            pltpu.VMEM((2, pairs, 16 * depth), jnp.bfloat16),
            pltpu.SemaphoreType.DMA,
        ],
        compiler_params=pltpu.CompilerParams(vmem_limit_bytes=40 * 2**20),
        cost_estimate=pl.CostEstimate(
            flops=4 * pairs * 2048 * cols, bytes_accessed=9 * 2**20, transcendentals=0
        ),
    )(place, *amps, core_swap(amps[1]), *swap_amps, core_swap(swap_amps[1]), block, partner, two, two_partner, up, down)


def solution(mesh):
    in_specs = (P("col", "row"), P("row", "col"), P("col", "row"))
    out_specs = P("row", "col")
    return jax.shard_map(
        on_device, mesh=mesh, in_specs=in_specs, out_specs=out_specs, check_vma=False
    )
```

```python
import jax
import jax.numpy as jnp
from jax import lax
from jax.experimental import pallas as pl
from jax.experimental.pallas import tpu as pltpu
from jax.sharding import PartitionSpec as P

OI = 4
Q = 4
FAR_GROUPS = [[(4 * q + m) * 2 + x for q in range(4)] for m in range(4) for x in range(2)]
TWO = [
    (r * 16 + c, (r + (4 if c % 2 == 0 else 28)) % 32 * 16 + c) for r in range(32) for c in range(16)
]
CORE_GROUPS = [list(range(c, 16, 2)) for c in range(2)]
CORE_PAIRS = [[2 * g, 2 * g + 1] for g in range(8)]
STEPS = (((0, 1), (0, 3)), ((0, 2), (1, 0)), ((1, 1), (1, 3)), ((1, 2), (1, 2)))
NTILE = 256


def z_shift(x, d):
    return lax.ppermute(x, "row", [(r, (r + 2 * d) % 32) for r in range(32)])


def x_swap(x):
    return lax.ppermute(x, "row", [(r, r ^ 1) for r in range(32)])


def core_swap(x):
    return lax.ppermute(x, "col", [(c, c ^ 1) for c in range(16)])


def chip_shift(x, step):
    pairs = []
    for xh in range(2):
        for y in range(4):
            for c in range(2):
                dx, dy = step[c]
                pairs.append(((xh * 4 + y) * 2 + c, ((xh ^ dx) * 4 + (y + dy) % 4) * 2 + c))
    return lax.ppermute(x, "col", pairs)


def gather_chips(x):
    chip = lax.all_gather(x, "col", axis=0, axis_index_groups=CORE_PAIRS)
    got = [chip_shift(chip, step) for step in STEPS[:3]]
    got.append(chip_shift(x, STEPS[3])[None])
    return chip, jnp.concatenate(got)


def products(place, *refs):
    z, xl, core, xh, y = (place[i] for i in range(5))
    amp_refs, blocks, (out, ints, amps, sem) = refs[:5], refs[5:11], refs[11:]
    near_own, near_swap, two, two_partner, up, down = blocks
    copies = []

    def amp_copy(ref, s, dx, dy, c):
        col = ((xh ^ dx) * 4 + ((y - dy) & 3)) * 2 + c
        lanes = pl.ds(pl.multiple_of(col * 128, 128), 128)
        copies.append((ref, amps.at[s, :, lanes]))

    chip, mine, theirs, swap_mine, swap_theirs = amp_refs
    for c in range(2):
        amp_copy(chip.at[c], 0, 0, 0, c)
    for ref, who in ((mine, core), (theirs, 1 - core)):
        for n, step in enumerate(STEPS):
            dx = jnp.where(who == 0, step[0][0], step[1][0])
            dy = jnp.where(who == 0, step[0][1], step[1][1])
            if n < 3:
                for c in range(2):
                    amp_copy(ref.at[2 * n + c], 0, dx, dy, c)
            else:
                amp_copy(ref.at[6], 0, dx, dy, who)
    for ref, who in ((swap_mine, core), (swap_theirs, 1 - core)):
        for g in range(8):
            lanes = pl.ds(pl.multiple_of((2 * g + who) * 128, 128), 128)
            copies.append((ref.at[g], amps.at[1, :, lanes]))
    for ref, shift, x_index in (
        (near_own, 0, xl),
        (near_swap, 0, 1 - xl),
        (two, 2, xl),
        (two_partner, 2, 1 - xl),
        (up.at[0], 3, xl),
        (up.at[1], 3, 1 - xl),
        (down.at[0], 1, xl),
        (down.at[1], 1, 1 - xl),
    ):
        copies.append((ref, ints.at[:, (z + shift) & 3, x_index]))
    copies = [pltpu.make_async_copy(a, b, sem) for a, b in copies]
    for copy in copies:
        copy.start()
    for copy in copies:
        copy.wait()

    def tile(n, carry):
        cols = pl.ds(pl.multiple_of(n * NTILE, NTILE), NTILE)
        right = ints[:, :, :, :, cols].reshape(-1, NTILE)
        total = jnp.dot(amps[0], right, preferred_element_type=jnp.float32) - jnp.dot(
            amps[1], right, preferred_element_type=jnp.float32
        )
        out[:, cols] = total.astype(out.dtype)
        return carry

    lax.fori_loop(0, out.shape[1] // NTILE, tile, 0)


def on_device(amplitudes, integrals, tile_mask):
    row, col = lax.axis_index("row"), lax.axis_index("col")
    place = jnp.stack([row // 2, row % 2, col % 2, col // 8, col // 2 % 4]).astype(jnp.int32)
    rows, cols = integrals.shape
    depth, pairs = amplitudes.shape

    copies = jnp.broadcast_to(integrals[None], (Q, rows, cols))
    block = lax.all_to_all(
        copies, "row", split_axis=0, concat_axis=0, tiled=True, axis_index_groups=FAR_GROUPS
    )

    scale = jnp.repeat(tile_mask.astype(jnp.bfloat16).reshape(-1), pairs // OI)
    masked = (amplitudes * scale[None, :]).T
    amps = gather_chips(masked)
    sent = masked.reshape(OI, 32, OI, depth).transpose(1, 2, 0, 3)
    sent, amps = lax.optimization_barrier((sent, amps))
    got = lax.all_to_all(sent, "row", split_axis=0, concat_axis=0, tiled=True)
    swapped = got.transpose(1, 0, 2, 3).reshape(pairs, depth)

    two = lax.ppermute(block, ("row", "col"), TWO)
    partner = x_swap(block)
    near = jnp.stack([block, partner])
    up = z_shift(near, 1)
    down = z_shift(near, -1)
    two_partner = x_swap(two)
    swapped, partner, two = lax.optimization_barrier((swapped, partner, two))
    spread = jnp.broadcast_to(swapped[None], (8, pairs, depth))
    own = lax.all_to_all(
        spread, "col", split_axis=0, concat_axis=0, tiled=True, axis_index_groups=CORE_GROUPS
    )

    anywhere = pl.BlockSpec(memory_space=pl.ANY)
    return pl.pallas_call(
        products,
        out_shape=jax.ShapeDtypeStruct((pairs, cols), jnp.bfloat16),
        in_specs=[pl.BlockSpec(memory_space=pltpu.SMEM)] + [anywhere] * 11,
        out_specs=pl.BlockSpec(memory_space=pltpu.VMEM),
        scratch_shapes=[
            pltpu.VMEM((Q, 4, 2, rows, cols), jnp.bfloat16),
            pltpu.VMEM((2, pairs, 16 * depth), jnp.bfloat16),
            pltpu.SemaphoreType.DMA,
        ],
        compiler_params=pltpu.CompilerParams(vmem_limit_bytes=40 * 2**20),
        cost_estimate=pl.CostEstimate(
            flops=4 * pairs * 2048 * cols, bytes_accessed=9 * 2**20, transcendentals=0
        ),
    )(place, *amps, core_swap(amps[1]), own, core_swap(own), block, partner, two, two_partner, up, down)


def solution(mesh):
    in_specs = (P("col", "row"), P("row", "col"), P("col", "row"))
    out_specs = P("row", "col")
    return jax.shard_map(
        on_device, mesh=mesh, in_specs=in_specs, out_specs=out_specs, check_vma=False
    )
```

```python
import jax
import jax.numpy as jnp
from jax import lax
from jax.experimental import pallas as pl
from jax.experimental.pallas import tpu as pltpu
from jax.sharding import PartitionSpec as P

OI = 4
Q = 4
FAR_GROUPS = [[(4 * q + m) * 2 + x for q in range(4)] for m in range(4) for x in range(2)]
TWO = [
    (r * 16 + c, (r + (4 if c % 2 == 0 else 28)) % 32 * 16 + c) for r in range(32) for c in range(16)
]
CORE_PAIRS = [[2 * g, 2 * g + 1] for g in range(8)]
STEPS = (((0, 1), (0, 3)), ((0, 2), (1, 0)), ((1, 1), (1, 3)), ((1, 2), (1, 2)))
NTILE = 256


def z_shift(x, d):
    return lax.ppermute(x, "row", [(r, (r + 2 * d) % 32) for r in range(32)])


def x_swap(x):
    return lax.ppermute(x, "row", [(r, r ^ 1) for r in range(32)])


def core_swap(x):
    return lax.ppermute(x, "col", [(c, c ^ 1) for c in range(16)])


def chip_shift(x, step):
    pairs = []
    for xh in range(2):
        for y in range(4):
            for c in range(2):
                dx, dy = step[c]
                pairs.append(((xh * 4 + y) * 2 + c, ((xh ^ dx) * 4 + (y + dy) % 4) * 2 + c))
    return lax.ppermute(x, "col", pairs)


def products(place, *refs):
    z, xl, core, xh, y = (place[i] for i in range(5))
    chip, mine, theirs, *blocks = refs[:11]
    out, ints, amps, total, early, late = refs[11:]
    first, second = [], []

    def amp_copy(ref, col):
        half = (col + z) & 1
        lanes = pl.ds(pl.multiple_of((col >> 1) * 128, 128), 128)
        for s in range(2):
            first.append((ref.at[s], amps.at[s, half, :, lanes]))

    for c in range(2):
        amp_copy(chip.at[c], (xh * 4 + y) * 2 + c)
    for ref, who in ((mine, core), (theirs, 1 - core)):
        for n, step in enumerate(STEPS):
            dx = jnp.where(who == 0, step[0][0], step[1][0])
            dy = jnp.where(who == 0, step[0][1], step[1][1])
            place_of = ((xh ^ dx) * 4 + ((y - dy) & 3)) * 2
            if n < 3:
                for c in range(2):
                    amp_copy(ref.at[2 * n + c], place_of + c)
            else:
                amp_copy(ref.at[6], place_of + who)
    for ref, shift, x_index in zip(
        blocks, (0, 0, 2, 2, 3, 3, 1, 1), (xl, 1 - xl, xl, 1 - xl, xl, 1 - xl, xl, 1 - xl)
    ):
        m = (z + shift) & 3
        pair = (ref, ints.at[shift & 1, :, m >> 1, x_index])
        (second if shift & 1 else first).append(pair)
    first = [pltpu.make_async_copy(a, b, early) for a, b in first]
    second = [pltpu.make_async_copy(a, b, late) for a, b in second]
    for copy in first + second:
        copy.start()

    def tile(half, n):
        cols = pl.ds(pl.multiple_of(n * NTILE, NTILE), NTILE)
        right = ints[half, :, :, :, :, cols].reshape(-1, NTILE)
        return cols, jnp.dot(
            amps[0, half], right, preferred_element_type=jnp.float32
        ) - jnp.dot(amps[1, half], right, preferred_element_type=jnp.float32)

    def begin(n, carry):
        cols, part = tile(0, n)
        total[:, cols] = part
        return carry

    def finish(n, carry):
        cols, part = tile(1, n)
        out[:, cols] = (total[:, cols] + part).astype(out.dtype)
        return carry

    for copy in first:
        copy.wait()
    lax.fori_loop(0, out.shape[1] // NTILE, begin, 0)
    for copy in second:
        copy.wait()
    lax.fori_loop(0, out.shape[1] // NTILE, finish, 0)


def on_device(amplitudes, integrals, tile_mask):
    row, col = lax.axis_index("row"), lax.axis_index("col")
    place = jnp.stack([row // 2, row % 2, col % 2, col // 8, col // 2 % 4]).astype(jnp.int32)
    rows, cols = integrals.shape
    depth, pairs = amplitudes.shape

    scale = jnp.repeat(tile_mask.astype(jnp.bfloat16).reshape(-1), pairs // OI)
    masked = (amplitudes * scale[None, :]).T

    sent = masked.reshape(OI, 32, OI, depth).transpose(1, 2, 0, 3)
    got = lax.all_to_all(sent, "row", split_axis=0, concat_axis=0, tiled=True)
    got, integrals = lax.optimization_barrier((got, integrals))
    swapped = got.transpose(1, 0, 2, 3).reshape(pairs, depth)

    copies = jnp.broadcast_to(integrals[None], (Q, rows, cols))
    block = lax.all_to_all(
        copies, "row", split_axis=0, concat_axis=0, tiled=True, axis_index_groups=FAR_GROUPS
    )

    both = jnp.stack([masked, swapped])
    chip = lax.all_gather(both, "col", axis=0, axis_index_groups=CORE_PAIRS)
    mine = [chip_shift(chip, step) for step in STEPS[:3]]
    mine.append(chip_shift(both, STEPS[3])[None])
    block, mine[:2] = lax.optimization_barrier((block, mine[:2]))
    mine = jnp.concatenate(mine)

    partner = x_swap(block)
    up = z_shift(block, 1)
    down = z_shift(block, -1)
    two = lax.ppermute(block, ("row", "col"), TWO)
    up_partner = z_shift(partner, 1)
    down_partner = z_shift(partner, -1)
    two_partner = x_swap(two)

    anywhere = pl.BlockSpec(memory_space=pl.ANY)
    return pl.pallas_call(
        products,
        out_shape=jax.ShapeDtypeStruct((pairs, cols), jnp.bfloat16),
        in_specs=[pl.BlockSpec(memory_space=pltpu.SMEM)] + [anywhere] * 11,
        out_specs=pl.BlockSpec(memory_space=pltpu.VMEM),
        scratch_shapes=[
            pltpu.VMEM((2, Q, 2, 2, rows, cols), jnp.bfloat16),
            pltpu.VMEM((2, 2, pairs, 8 * depth), jnp.bfloat16),
            pltpu.VMEM((pairs, cols), jnp.float32),
            pltpu.SemaphoreType.DMA,
            pltpu.SemaphoreType.DMA,
        ],
        compiler_params=pltpu.CompilerParams(vmem_limit_bytes=40 * 2**20),
        cost_estimate=pl.CostEstimate(
            flops=4 * pairs * 2048 * cols, bytes_accessed=9 * 2**20, transcendentals=0
        ),
    )(
        place,
        chip,
        mine,
        core_swap(mine),
        block,
        partner,
        two,
        two_partner,
        up,
        up_partner,
        down,
        down_partner,
    )


def solution(mesh):
    in_specs = (P("col", "row"), P("row", "col"), P("col", "row"))
    out_specs = P("row", "col")
    return jax.shard_map(
        on_device, mesh=mesh, in_specs=in_specs, out_specs=out_specs, check_vma=False
    )
```

```python
import jax
import jax.numpy as jnp
from jax import lax
from jax.experimental import pallas as pl
from jax.experimental.pallas import tpu as pltpu
from jax.sharding import PartitionSpec as P

OI = 4
Q = 4
FAR_GROUPS = [[(4 * q + m) * 2 + x for q in range(4)] for m in range(4) for x in range(2)]
TWO = [
    (r * 16 + c, (r + (4 if c % 2 == 0 else 28)) % 32 * 16 + c) for r in range(32) for c in range(16)
]
CORE_PAIRS = [[2 * g, 2 * g + 1] for g in range(8)]
STEPS = (((0, 1), (0, 3)), ((0, 2), (1, 0)), ((1, 1), (1, 3)), ((1, 2), (1, 2)))
NTILE = 256


def z_shift(x, d):
    return lax.ppermute(x, "row", [(r, (r + 2 * d) % 32) for r in range(32)])


def x_swap(x):
    return lax.ppermute(x, "row", [(r, r ^ 1) for r in range(32)])


def core_swap(x):
    return lax.ppermute(x, "col", [(c, c ^ 1) for c in range(16)])


def chip_shift(x, step):
    pairs = []
    for xh in range(2):
        for y in range(4):
            for c in range(2):
                dx, dy = step[c]
                pairs.append(((xh * 4 + y) * 2 + c, ((xh ^ dx) * 4 + (y + dy) % 4) * 2 + c))
    return lax.ppermute(x, "col", pairs)


def multiply(amps, ints, cols):
    right = ints[:, :, :, :, cols].reshape(-1, NTILE)
    return jnp.dot(amps[0], right, preferred_element_type=jnp.float32) - jnp.dot(
        amps[1], right, preferred_element_type=jnp.float32
    )


def columns(n):
    return pl.ds(pl.multiple_of(n * NTILE, NTILE), NTILE)


def block_copies(place, refs, shifts, ints):
    z, xl = place[0], place[1]
    copies = []
    for ref, partner, shift in zip(refs[::2], refs[1::2], shifts):
        m = (z + shift) & 3
        copies.append((ref, ints.at[:, m >> 1, xl]))
        copies.append((partner, ints.at[:, m >> 1, 1 - xl]))
    return copies


def run_copies(copies, sem):
    copies = [pltpu.make_async_copy(a, b, sem) for a, b in copies]
    for copy in copies:
        copy.start()
    for copy in copies:
        copy.wait()


def first_half(place, whole, chip, mine, theirs, *refs):
    z, core, xh, y = place[0], place[2], place[3], place[4]
    blocks, (total, kept, ints, sem) = refs[:4], refs[4:]
    copies = block_copies(place, blocks, (0, 2), ints)
    for k in range(8):
        lanes = pl.ds(k * 128, 128)
        for half in range(2):
            copies.append((whole.at[2 * k + ((z + half) & 1)], kept.at[half, 0, :, lanes]))
    swaps = []
    for c in range(2):
        swaps.append((chip.at[c], (xh * 4 + y) * 2 + c))
    for ref, who in ((mine, core), (theirs, 1 - core)):
        for n, step in enumerate(STEPS):
            dx = jnp.where(who == 0, step[0][0], step[1][0])
            dy = jnp.where(who == 0, step[0][1], step[1][1])
            place_of = ((xh ^ dx) * 4 + ((y - dy) & 3)) * 2
            if n < 3:
                for c in range(2):
                    swaps.append((ref.at[2 * n + c], place_of + c))
            else:
                swaps.append((ref.at[6], place_of + who))
    for ref, col in swaps:
        lanes = pl.ds(pl.multiple_of((col >> 1) * 128, 128), 128)
        copies.append((ref, kept.at[(col + z) & 1, 1, :, lanes]))
    run_copies(copies, sem)

    def tile(n, carry):
        cols = columns(n)
        total[:, cols] = multiply(kept.at[0], ints, cols)
        return carry

    lax.fori_loop(0, total.shape[1] // NTILE, tile, 0)


def second_half(place, total, kept, *refs):
    blocks, (out, ints, sem) = refs[:4], refs[4:]
    run_copies(block_copies(place, blocks, (1, 3), ints), sem)

    def tile(n, carry):
        cols = columns(n)
        out[:, cols] = (total[:, cols] + multiply(kept.at[1], ints, cols)).astype(out.dtype)
        return carry

    lax.fori_loop(0, out.shape[1] // NTILE, tile, 0)


def on_device(amplitudes, integrals, tile_mask):
    row, col = lax.axis_index("row"), lax.axis_index("col")
    place = jnp.stack([row // 2, row % 2, col % 2, col // 8, col // 2 % 4]).astype(jnp.int32)
    rows, cols = integrals.shape
    depth, pairs = amplitudes.shape

    scale = jnp.repeat(tile_mask.astype(jnp.bfloat16).reshape(-1), pairs // OI)
    masked = (amplitudes * scale[None, :]).T

    sent = masked.reshape(OI, 32, OI, depth).transpose(1, 2, 0, 3)
    got = lax.all_to_all(sent, "row", split_axis=0, concat_axis=0, tiled=True)
    got, integrals = lax.optimization_barrier((got, integrals))
    swapped = got.transpose(1, 0, 2, 3).reshape(pairs, depth)

    copies = jnp.broadcast_to(integrals[None], (Q, rows, cols))
    block = lax.all_to_all(
        copies, "row", split_axis=0, concat_axis=0, tiled=True, axis_index_groups=FAR_GROUPS
    )

    whole = lax.all_gather(masked, "col", axis=0)
    chip = lax.all_gather(swapped, "col", axis=0, axis_index_groups=CORE_PAIRS)
    mine = [chip_shift(chip, step) for step in STEPS[:3]]
    mine.append(chip_shift(swapped, STEPS[3])[None])
    mine = jnp.concatenate(mine)
    block, mine = lax.optimization_barrier((block, mine))

    partner = x_swap(block)
    two = lax.ppermute(block, ("row", "col"), TWO)
    up = z_shift(block, 1)
    down = z_shift(block, -1)
    up_partner = z_shift(partner, 1)
    down_partner = z_shift(partner, -1)
    two_partner = x_swap(two)

    anywhere = pl.BlockSpec(memory_space=pl.ANY)
    scalars = pl.BlockSpec(memory_space=pltpu.SMEM)
    vector = pl.BlockSpec(memory_space=pltpu.VMEM)
    ints = pltpu.VMEM((Q, 2, 2, rows, cols), jnp.bfloat16)
    params = pltpu.CompilerParams(vmem_limit_bytes=32 * 2**20)
    cost = pl.CostEstimate(
        flops=2 * pairs * 2048 * cols, bytes_accessed=10 * 2**20, transcendentals=0
    )
    total, kept = pl.pallas_call(
        first_half,
        out_shape=(
            jax.ShapeDtypeStruct((pairs, cols), jnp.float32),
            jax.ShapeDtypeStruct((2, 2, pairs, 8 * depth), jnp.bfloat16),
        ),
        in_specs=[scalars] + [anywhere] * 8,
        out_specs=(vector, vector),
        scratch_shapes=[ints, pltpu.SemaphoreType.DMA],
        compiler_params=params,
        cost_estimate=cost,
    )(place, whole, chip, mine, core_swap(mine), block, partner, two, two_partner)
    return pl.pallas_call(
        second_half,
        out_shape=jax.ShapeDtypeStruct((pairs, cols), jnp.bfloat16),
        in_specs=[scalars, vector, vector] + [anywhere] * 4,
        out_specs=vector,
        scratch_shapes=[ints, pltpu.SemaphoreType.DMA],
        compiler_params=params,
        cost_estimate=cost,
    )(place, total, kept, down, down_partner, up, up_partner)


def solution(mesh):
    in_specs = (P("col", "row"), P("row", "col"), P("col", "row"))
    out_specs = P("row", "col")
    return jax.shard_map(
        on_device, mesh=mesh, in_specs=in_specs, out_specs=out_specs, check_vma=False
    )
```

```python
import jax
import jax.numpy as jnp
from jax import lax
from jax.experimental import pallas as pl
from jax.experimental.pallas import tpu as pltpu
from jax.sharding import PartitionSpec as P

OI = 4
FAR = (0, -4, 4, 8)
TWO = [
    (r * 16 + c, (r + (4 if c % 2 == 0 else 28)) % 32 * 16 + c) for r in range(32) for c in range(16)
]
CORE_PAIRS = [[2 * g, 2 * g + 1] for g in range(8)]
STEPS = (((0, 1), (0, 3)), ((0, 2), (1, 0)), ((1, 1), (1, 3)), ((1, 2), (1, 2)))
NTILE = 256


def z_shift(x, d):
    return lax.ppermute(x, "row", [(r, (r + 2 * d) % 32) for r in range(32)])


def x_swap(x):
    return lax.ppermute(x, "row", [(r, r ^ 1) for r in range(32)])


def core_swap(x):
    return lax.ppermute(x, "col", [(c, c ^ 1) for c in range(16)])


def chip_shift(x, step):
    pairs = []
    for xh in range(2):
        for y in range(4):
            for c in range(2):
                dx, dy = step[c]
                pairs.append(((xh * 4 + y) * 2 + c, ((xh ^ dx) * 4 + (y + dy) % 4) * 2 + c))
    return lax.ppermute(x, "col", pairs)


def multiply(amps, ints, cols):
    right = ints[:, :, :, cols].reshape(-1, NTILE)
    return jnp.dot(amps[0], right, preferred_element_type=jnp.float32) - jnp.dot(
        amps[1], right, preferred_element_type=jnp.float32
    )


def columns(n):
    return pl.ds(pl.multiple_of(n * NTILE, NTILE), NTILE)


def block_copies(place, refs, shifts, ints):
    z, xl = place[0], place[1]
    copies = []
    for ref, partner, shift in zip(refs[::2], refs[1::2], shifts):
        for slot, offset in enumerate(FAR):
            k = (z + shift + offset) & 15
            copies.append((ref.at[slot], ints.at[k >> 1, xl]))
            copies.append((partner.at[slot], ints.at[k >> 1, 1 - xl]))
    return copies


def run_copies(copies, sem):
    copies = [pltpu.make_async_copy(a, b, sem) for a, b in copies]
    for copy in copies:
        copy.start()
    for copy in copies:
        copy.wait()


def first_half(place, chip, *refs):
    z, core, xh, y = place[0], place[2], place[3], place[4]
    mine, theirs, blocks = refs[:4], refs[4:8], refs[8:12]
    total, kept, ints, sem = refs[12:]
    copies = block_copies(place, blocks, (0, 4 * core - 2), ints)
    shards = [(chip.at[c], (xh * 4 + y) * 2 + c) for c in range(2)]
    for refs, who in ((mine, core), (theirs, 1 - core)):
        for n, step in enumerate(STEPS):
            dx = jnp.where(who == 0, step[0][0], step[1][0])
            dy = jnp.where(who == 0, step[0][1], step[1][1])
            place_of = ((xh ^ dx) * 4 + ((y - dy) & 3)) * 2
            if n < 3:
                for c in range(2):
                    shards.append((refs[n].at[c], place_of + c))
            else:
                shards.append((refs[n].at[0], place_of + who))
    for ref, col in shards:
        lanes = pl.ds(pl.multiple_of((col >> 1) * 128, 128), 128)
        for s in range(2):
            copies.append((ref.at[s], kept.at[(col + z) & 1, s, :, lanes]))
    run_copies(copies, sem)

    def tile(n, carry):
        cols = columns(n)
        total[:, cols] = multiply(kept.at[0], ints, cols)
        return carry

    lax.fori_loop(0, total.shape[1] // NTILE, tile, 0)


def second_half(place, total, kept, *refs):
    blocks = [refs[i].at[x] for i in range(2) for x in range(2)]
    out, ints, sem = refs[2:]
    run_copies(block_copies(place, blocks, (1, -1), ints), sem)

    def tile(n, carry):
        cols = columns(n)
        out[:, cols] = (total[:, cols] + multiply(kept.at[1], ints, cols)).astype(out.dtype)
        return carry

    lax.fori_loop(0, out.shape[1] // NTILE, tile, 0)


def on_device(amplitudes, integrals, tile_mask):
    row, col = lax.axis_index("row"), lax.axis_index("col")
    place = jnp.stack([row // 2, row % 2, col % 2, col // 8, col // 2 % 4]).astype(jnp.int32)
    rows, cols = integrals.shape
    depth, pairs = amplitudes.shape

    far = z_shift(integrals, 8)
    block = jnp.stack([integrals, z_shift(integrals, 4), z_shift(integrals, -4), far])

    scale = jnp.repeat(tile_mask.astype(jnp.bfloat16).reshape(-1), pairs // OI)
    masked = (amplitudes * scale[None, :]).T

    sent = masked.reshape(OI, 32, OI, depth).transpose(1, 2, 0, 3)
    got = lax.all_to_all(sent, "row", split_axis=0, concat_axis=0, tiled=True)
    swapped = got.transpose(1, 0, 2, 3).reshape(pairs, depth)
    swapped, block = lax.optimization_barrier((swapped, block))

    both = jnp.stack([masked, swapped])
    chip = lax.all_gather(both, "col", axis=0, axis_index_groups=CORE_PAIRS)
    mine = [chip_shift(chip, step) for step in STEPS[:3]]

    partner = x_swap(block)
    two = lax.ppermute(block, ("row", "col"), TWO)
    both, partner, two = lax.optimization_barrier((both, partner, two))
    mine.append(chip_shift(both, STEPS[3])[None])
    theirs = [core_swap(m) for m in mine]
    near = jnp.stack([block, partner])
    up = z_shift(near, 1)
    down = z_shift(near, -1)
    two_partner = x_swap(two)

    anywhere = pl.BlockSpec(memory_space=pl.ANY)
    scalars = pl.BlockSpec(memory_space=pltpu.SMEM)
    vector = pl.BlockSpec(memory_space=pltpu.VMEM)
    ints = pltpu.VMEM((8, 2, rows, cols), jnp.bfloat16)
    params = pltpu.CompilerParams(vmem_limit_bytes=32 * 2**20)
    cost = pl.CostEstimate(
        flops=2 * pairs * 2048 * cols, bytes_accessed=10 * 2**20, transcendentals=0
    )
    total, kept = pl.pallas_call(
        first_half,
        out_shape=(
            jax.ShapeDtypeStruct((pairs, cols), jnp.float32),
            jax.ShapeDtypeStruct((2, 2, pairs, 8 * depth), jnp.bfloat16),
        ),
        in_specs=[scalars] + [anywhere] * 13,
        out_specs=(vector, vector),
        scratch_shapes=[ints, pltpu.SemaphoreType.DMA],
        compiler_params=params,
        cost_estimate=cost,
    )(place, chip, *mine, *theirs, block, partner, two, two_partner)
    return pl.pallas_call(
        second_half,
        out_shape=jax.ShapeDtypeStruct((pairs, cols), jnp.bfloat16),
        in_specs=[scalars, vector, vector] + [anywhere] * 2,
        out_specs=vector,
        scratch_shapes=[ints, pltpu.SemaphoreType.DMA],
        compiler_params=params,
        cost_estimate=cost,
    )(place, total, kept, down, up)


def solution(mesh):
    in_specs = (P("col", "row"), P("row", "col"), P("col", "row"))
    out_specs = P("row", "col")
    return jax.shard_map(
        on_device, mesh=mesh, in_specs=in_specs, out_specs=out_specs, check_vma=False
    )
```

```python
import jax
import jax.numpy as jnp
from jax import lax
from jax.experimental import pallas as pl
from jax.experimental.pallas import tpu as pltpu
from jax.sharding import PartitionSpec as P

OI = 4
NTILE = 256


def z_shift(x, d):
    return lax.ppermute(x, "row", [(r, (r + 2 * d) % 32) for r in range(32)])


def split_shift(d):
    step = (2 * d, 32 - 2 * d)
    return [(r * 16 + c, (r + step[c % 2]) % 32 * 16 + c) for r in range(32) for c in range(16)]


def x_swap(x):
    return lax.ppermute(x, "row", [(r, r ^ 1) for r in range(32)])


def core_swap(x):
    return lax.ppermute(x, "col", [(c, c ^ 1) for c in range(16)])


def chip_shift(x, step):
    dx, dy = step
    return lax.ppermute(
        x, "col", [(c, (c // 8 ^ dx) * 8 + (c // 2 % 4 + dy) % 4 * 2 + c % 2) for c in range(16)]
    )


def multiply(amps, ints, cols):
    right = ints[:, :, :, :, cols].reshape(-1, NTILE)
    return jnp.dot(amps[0], right, preferred_element_type=jnp.float32) - jnp.dot(
        amps[1], right, preferred_element_type=jnp.float32
    )


def columns(n):
    return pl.ds(pl.multiple_of(n * NTILE, NTILE), NTILE)


def block_copies(place, refs, shifts, ints):
    z, xl = place[0], place[1]
    copies = []
    for ref, partner, shift in zip(refs[::2], refs[1::2], shifts):
        m = (z + shift) & 3
        copies.append((ref, ints.at[:, m >> 1, xl]))
        copies.append((partner, ints.at[:, m >> 1, 1 - xl]))
    return copies


def run_copies(copies, sem):
    copies = [pltpu.make_async_copy(a, b, sem) for a, b in copies]
    for copy in copies:
        copy.start()
    for copy in copies:
        copy.wait()


def four(place, here, below, above, far, out):
    q = place[0] >> 2
    for step, shard in enumerate((here, above, far, below)):
        out[(q + step) & 3] = shard[...]


def gather_four(place, *shards):
    return pl.pallas_call(
        four,
        out_shape=jax.ShapeDtypeStruct((4,) + shards[0].shape, shards[0].dtype),
        in_specs=[pl.BlockSpec(memory_space=pltpu.SMEM)]
        + [pl.BlockSpec(memory_space=pltpu.VMEM)] * 4,
        out_specs=pl.BlockSpec(memory_space=pltpu.VMEM),
    )(place, *shards)


def first_half(place, *refs):
    z, core, xh, y = place[0], place[2], place[3], place[4]
    mine, theirs, blocks = refs[:4], refs[4:8], refs[8:12]
    total, kept, ints, sem = refs[12:]
    copies = block_copies(place, blocks, (0, 2), ints)
    shards = []
    for refs, who in ((mine, core), (theirs, 1 - core)):
        for ref, dy in zip(refs, (0, 1, 3, 2)):
            for dx in range(2):
                shards.append((ref.at[dx], ((xh ^ dx) * 4 + ((y - dy) & 3)) * 2 + who))
    for ref, col in shards:
        lanes = pl.ds(pl.multiple_of((col >> 1) * 128, 128), 128)
        for s in range(2):
            copies.append((ref.at[s], kept.at[(col + z) & 1, s, :, lanes]))
    run_copies(copies, sem)

    def tile(n, carry):
        cols = columns(n)
        total[:, cols] = multiply(kept.at[0], ints, cols)
        return carry

    lax.fori_loop(0, total.shape[1] // NTILE, tile, 0)


def second_half(place, total, kept, *refs):
    blocks = [refs[i].at[x] for i in range(2) for x in range(2)]
    out, ints, sem = refs[2:]
    run_copies(block_copies(place, blocks, (1, -1), ints), sem)

    def tile(n, carry):
        cols = columns(n)
        out[:, cols] = (total[:, cols] + multiply(kept.at[1], ints, cols)).astype(out.dtype)
        return carry

    lax.fori_loop(0, out.shape[1] // NTILE, tile, 0)


def on_device(amplitudes, integrals, tile_mask):
    row, col = lax.axis_index("row"), lax.axis_index("col")
    core = col % 2
    place = jnp.stack([row // 2, row % 2, core, col // 8, col // 2 % 4]).astype(jnp.int32)
    rows, cols = integrals.shape
    depth, pairs = amplitudes.shape

    up4 = z_shift(integrals, 4)
    down4 = z_shift(integrals, -4)
    far = lax.ppermute(jnp.where(core == 0, up4, down4), ("row", "col"), split_shift(4))

    scale = jnp.repeat(tile_mask.astype(jnp.bfloat16).reshape(-1), pairs // OI)
    masked = (amplitudes * scale[None, :]).T

    masked, up4, down4 = lax.optimization_barrier((masked, up4, down4))
    sent = masked.reshape(OI, 32, OI, depth).transpose(1, 2, 0, 3)
    got = lax.all_to_all(sent, "row", split_axis=0, concat_axis=0, tiled=True)
    swapped = got.transpose(1, 0, 2, 3).reshape(pairs, depth)
    block = gather_four(place, integrals, up4, down4, far)
    swapped, block = lax.optimization_barrier((swapped, block))

    both = jnp.stack([masked, swapped])
    pair = jnp.stack([both, chip_shift(both, (1, 0))])
    mine = [pair] + [chip_shift(pair, (0, dy)) for dy in (1, 3)]

    partner = x_swap(block)
    two = lax.ppermute(block, ("row", "col"), split_shift(2))
    pair, partner, two = lax.optimization_barrier((pair, partner, two))
    mine.append(chip_shift(pair, (0, 2)))
    theirs = [core_swap(m) for m in mine]
    near = jnp.stack([block, partner])
    up = z_shift(near, 1)
    down = z_shift(near, -1)
    two_partner = x_swap(two)

    anywhere = pl.BlockSpec(memory_space=pl.ANY)
    scalars = pl.BlockSpec(memory_space=pltpu.SMEM)
    vector = pl.BlockSpec(memory_space=pltpu.VMEM)
    ints = pltpu.VMEM((4, 2, 2, rows, cols), jnp.bfloat16)
    params = pltpu.CompilerParams(vmem_limit_bytes=32 * 2**20)
    cost = pl.CostEstimate(
        flops=2 * pairs * 2048 * cols, bytes_accessed=10 * 2**20, transcendentals=0
    )
    total, kept = pl.pallas_call(
        first_half,
        out_shape=(
            jax.ShapeDtypeStruct((pairs, cols), jnp.float32),
            jax.ShapeDtypeStruct((2, 2, pairs, 8 * depth), jnp.bfloat16),
        ),
        in_specs=[scalars] + [anywhere] * 12,
        out_specs=(vector, vector),
        scratch_shapes=[ints, pltpu.SemaphoreType.DMA],
        compiler_params=params,
        cost_estimate=cost,
    )(place, *mine, *theirs, block, partner, two, two_partner)
    return pl.pallas_call(
        second_half,
        out_shape=jax.ShapeDtypeStruct((pairs, cols), jnp.bfloat16),
        in_specs=[scalars, vector, vector] + [anywhere] * 2,
        out_specs=vector,
        scratch_shapes=[ints, pltpu.SemaphoreType.DMA],
        compiler_params=params,
        cost_estimate=cost,
    )(place, total, kept, down, up)


def solution(mesh):
    in_specs = (P("col", "row"), P("row", "col"), P("col", "row"))
    out_specs = P("row", "col")
    return jax.shard_map(
        on_device, mesh=mesh, in_specs=in_specs, out_specs=out_specs, check_vma=False
    )
```

```python
import jax
import jax.numpy as jnp
from jax import lax
from jax.experimental import pallas as pl
from jax.experimental.pallas import tpu as pltpu
from jax.sharding import PartitionSpec as P

OI = 4
NTILE = 256


def z_shift(x, d):
    return lax.ppermute(x, "row", [(r, (r + 2 * d) % 32) for r in range(32)])


def split_shift(d):
    step = (2 * d, 32 - 2 * d)
    return [(r * 16 + c, (r + step[c % 2]) % 32 * 16 + c) for r in range(32) for c in range(16)]


def x_swap(x):
    return lax.ppermute(x, "row", [(r, r ^ 1) for r in range(32)])


def core_swap(x):
    return lax.ppermute(x, "col", [(c, c ^ 1) for c in range(16)])


def chip_shift(x, step):
    dx, dy = step
    return lax.ppermute(
        x, "col", [(c, (c // 8 ^ dx) * 8 + (c // 2 % 4 + dy) % 4 * 2 + c % 2) for c in range(16)]
    )


def multiply(amps, ints, cols):
    right = ints[:, :, :, :, cols].reshape(-1, NTILE)
    return jnp.dot(amps[0], right, preferred_element_type=jnp.float32) - jnp.dot(
        amps[1], right, preferred_element_type=jnp.float32
    )


def columns(n):
    return pl.ds(pl.multiple_of(n * NTILE, NTILE), NTILE)


def block_copies(place, refs, shifts, ints):
    z, xl = place[0], place[1]
    copies = []
    for ref, partner, shift in zip(refs[::2], refs[1::2], shifts):
        m = (z + shift) & 3
        copies.append((ref, ints.at[:, m >> 1, xl]))
        copies.append((partner, ints.at[:, m >> 1, 1 - xl]))
    return copies


def run_copies(copies, sem):
    copies = [pltpu.make_async_copy(a, b, sem) for a, b in copies]
    for copy in copies:
        copy.start()
    for copy in copies:
        copy.wait()


def four(place, here, below, above, far, out):
    q = place[0] >> 2
    for step, shard in enumerate((here, above, far, below)):
        out[(q + step) & 3] = shard[...]


def gather_four(place, *shards):
    return pl.pallas_call(
        four,
        out_shape=jax.ShapeDtypeStruct((4,) + shards[0].shape, shards[0].dtype),
        in_specs=[pl.BlockSpec(memory_space=pltpu.SMEM)]
        + [pl.BlockSpec(memory_space=pltpu.VMEM)] * 4,
        out_specs=pl.BlockSpec(memory_space=pltpu.VMEM),
    )(place, *shards)


def first_half(place, *refs):
    z, core, xh, y = place[0], place[2], place[3], place[4]
    mine, theirs, blocks = refs[:4], refs[4:8], refs[8:12]
    total, kept, ints, sem = refs[12:]
    copies = block_copies(place, blocks, (0, 2), ints)
    shards = []
    for refs, who in ((mine, core), (theirs, 1 - core)):
        for ref, dy in zip(refs, (0, 1, 3, 2)):
            for dx in range(2):
                shards.append((ref.at[dx], ((xh ^ dx) * 4 + ((y - dy) & 3)) * 2 + who))
    for ref, col in shards:
        lanes = pl.ds(pl.multiple_of((col >> 1) * 128, 128), 128)
        for s in range(2):
            copies.append((ref.at[s], kept.at[(col + z) & 1, s, :, lanes]))
    run_copies(copies, sem)

    def tile(n, carry):
        cols = columns(n)
        total[:, cols] = multiply(kept.at[0], ints, cols)
        return carry

    lax.fori_loop(0, total.shape[1] // NTILE, tile, 0)


def second_half(place, total, kept, *refs):
    blocks = [refs[i].at[x] for i in range(2) for x in range(2)]
    out, ints, sem = refs[2:]
    run_copies(block_copies(place, blocks, (1, -1), ints), sem)

    def tile(n, carry):
        cols = columns(n)
        out[:, cols] = (total[:, cols] + multiply(kept.at[1], ints, cols)).astype(out.dtype)
        return carry

    lax.fori_loop(0, out.shape[1] // NTILE, tile, 0)


def on_device(amplitudes, integrals, tile_mask):
    row, col = lax.axis_index("row"), lax.axis_index("col")
    core = col % 2
    place = jnp.stack([row // 2, row % 2, core, col // 8, col // 2 % 4]).astype(jnp.int32)
    rows, cols = integrals.shape
    depth, pairs = amplitudes.shape

    up4 = z_shift(integrals, 4)
    down4 = z_shift(integrals, -4)
    far = lax.ppermute(jnp.where(core == 0, up4, down4), ("row", "col"), split_shift(4))

    scale = jnp.repeat(tile_mask.astype(jnp.bfloat16).reshape(-1), pairs // OI)
    masked = (amplitudes * scale[None, :]).T

    sent = masked.reshape(OI, 32, OI, depth).transpose(1, 2, 0, 3)
    got = lax.all_to_all(sent, "row", split_axis=0, concat_axis=0, tiled=True)
    swapped = got.transpose(1, 0, 2, 3).reshape(pairs, depth)
    swapped, up4, down4 = lax.optimization_barrier((swapped, up4, down4))
    block = gather_four(place, integrals, up4, down4, far)

    both = jnp.stack([masked, swapped])
    pair = jnp.stack([both, chip_shift(both, (1, 0))])
    mine = [pair] + [chip_shift(pair, (0, dy)) for dy in (1, 3)]

    partner = x_swap(block)
    two = lax.ppermute(block, ("row", "col"), split_shift(2))
    mine.append(chip_shift(pair, (0, 2)))
    theirs = [core_swap(m) for m in mine]
    near = jnp.stack([block, partner])
    up = z_shift(near, 1)
    down = z_shift(near, -1)
    two_partner = x_swap(two)

    anywhere = pl.BlockSpec(memory_space=pl.ANY)
    scalars = pl.BlockSpec(memory_space=pltpu.SMEM)
    vector = pl.BlockSpec(memory_space=pltpu.VMEM)
    ints = pltpu.VMEM((4, 2, 2, rows, cols), jnp.bfloat16)
    params = pltpu.CompilerParams(vmem_limit_bytes=32 * 2**20)
    cost = pl.CostEstimate(
        flops=2 * pairs * 2048 * cols, bytes_accessed=10 * 2**20, transcendentals=0
    )
    total, kept = pl.pallas_call(
        first_half,
        out_shape=(
            jax.ShapeDtypeStruct((pairs, cols), jnp.float32),
            jax.ShapeDtypeStruct((2, 2, pairs, 8 * depth), jnp.bfloat16),
        ),
        in_specs=[scalars] + [anywhere] * 12,
        out_specs=(vector, vector),
        scratch_shapes=[ints, pltpu.SemaphoreType.DMA],
        compiler_params=params,
        cost_estimate=cost,
    )(place, *mine, *theirs, block, partner, two, two_partner)
    return pl.pallas_call(
        second_half,
        out_shape=jax.ShapeDtypeStruct((pairs, cols), jnp.bfloat16),
        in_specs=[scalars, vector, vector] + [anywhere] * 2,
        out_specs=vector,
        scratch_shapes=[ints, pltpu.SemaphoreType.DMA],
        compiler_params=params,
        cost_estimate=cost,
    )(place, total, kept, down, up)


def solution(mesh):
    in_specs = (P("col", "row"), P("row", "col"), P("col", "row"))
    out_specs = P("row", "col")
    return jax.shard_map(
        on_device, mesh=mesh, in_specs=in_specs, out_specs=out_specs, check_vma=False
    )
```

```python
import functools

import jax
import jax.numpy as jnp
from jax import lax
from jax.experimental import pallas as pl
from jax.experimental.pallas import tpu as pltpu
from jax.sharding import PartitionSpec as P

OI = 4
NTILE = 256


def z_shift(x, d):
    return lax.ppermute(x, "row", [(r, (r + 2 * d) % 32) for r in range(32)])


def split_shift(d):
    step = (2 * d, 32 - 2 * d)
    return [(r * 16 + c, (r + step[c % 2]) % 32 * 16 + c) for r in range(32) for c in range(16)]


def x_swap(x):
    return lax.ppermute(x, "row", [(r, r ^ 1) for r in range(32)])


def core_swap(x):
    return lax.ppermute(x, "col", [(c, c ^ 1) for c in range(16)])


def chip_shift(x, step):
    dx, dy = step
    return lax.ppermute(
        x, "col", [(c, (c // 8 ^ dx) * 8 + (c // 2 % 4 + dy) % 4 * 2 + c % 2) for c in range(16)]
    )


def multiply(amps, ints, cols):
    right = ints[:, :, :, :, cols].reshape(-1, NTILE)
    return jnp.dot(amps[0], right, preferred_element_type=jnp.float32) - jnp.dot(
        amps[1], right, preferred_element_type=jnp.float32
    )


def columns(n):
    return pl.ds(pl.multiple_of(n * NTILE, NTILE), NTILE)


def block_copies(place, refs, shifts, ints):
    z, xl = place[0], place[1]
    copies = []
    for ref, partner, shift in zip(refs[::2], refs[1::2], shifts):
        m = (z + shift) & 3
        copies.append((ref, ints.at[m >> 1, :, xl]))
        copies.append((partner, ints.at[m >> 1, :, 1 - xl]))
    return copies


def run_copies(copies, sem):
    copies = [pltpu.make_async_copy(a, b, sem) for a, b in copies]
    for copy in copies:
        copy.start()
    for copy in copies:
        copy.wait()


def four(place, here, below, above, far, out):
    q = place[0] >> 2
    for step, shard in enumerate((here, above, far, below)):
        out[(q + step) & 3] = shard[...]


def gather_four(place, *shards):
    return pl.pallas_call(
        four,
        out_shape=jax.ShapeDtypeStruct((4,) + shards[0].shape, shards[0].dtype),
        in_specs=[pl.BlockSpec(memory_space=pltpu.SMEM)]
        + [pl.BlockSpec(memory_space=pltpu.VMEM)] * 4,
        out_specs=pl.BlockSpec(memory_space=pltpu.VMEM),
    )(place, *shards)


def first_half(place, *refs):
    z, core, xh, y = place[0], place[2], place[3], place[4]
    mine, theirs, blocks = refs[:4], refs[4:8], refs[8:12]
    total, kept, ints, sem = refs[12:]
    copies = block_copies(place, blocks, (0, 2), ints)
    shards = []
    for refs, who in ((mine, core), (theirs, 1 - core)):
        for ref, dy in zip(refs, (0, 1, 3, 2)):
            for dx in range(2):
                shards.append((ref.at[dx], ((xh ^ dx) * 4 + ((y - dy) & 3)) * 2 + who))
    for ref, col in shards:
        slot = ((col >> 1) & 1) * 4 + (col >> 2)
        lanes = pl.ds(pl.multiple_of(slot * 128, 128), 128)
        for s in range(2):
            copies.append((ref.at[s], kept.at[(col + z) & 1, s, :, lanes]))
    run_copies(copies, sem)

    def tile(n, carry):
        cols = columns(n)
        total[:, cols] = multiply(kept.at[0], ints, cols)
        return carry

    lax.fori_loop(0, total.shape[1] // NTILE, tile, 0)


def add_neighbour(shift, place, total, kept, block, out, ints, sem):
    z, xl = place[0], place[1]
    run_copies([(block.at[0], ints.at[0, :, xl]), (block.at[1], ints.at[0, :, 1 - xl])], sem)
    depth = kept.shape[3] // 2
    lanes = pl.ds(pl.multiple_of((((z + shift) & 3) >> 1) * depth, depth), depth)

    def tile(n, carry):
        cols = columns(n)
        amps = [kept[1, s, :, lanes] for s in range(2)]
        out[:, cols] = (total[:, cols] + multiply(amps, ints, cols)).astype(out.dtype)
        return carry

    lax.fori_loop(0, out.shape[1] // NTILE, tile, 0)


def on_device(amplitudes, integrals, tile_mask):
    row, col = lax.axis_index("row"), lax.axis_index("col")
    core = col % 2
    place = jnp.stack([row // 2, row % 2, core, col // 8, col // 2 % 4]).astype(jnp.int32)
    rows, cols = integrals.shape
    depth, pairs = amplitudes.shape

    up4 = z_shift(integrals, 4)
    down4 = z_shift(integrals, -4)
    far = lax.ppermute(jnp.where(core == 0, up4, down4), ("row", "col"), split_shift(4))

    scale = jnp.repeat(tile_mask.astype(jnp.bfloat16).reshape(-1), pairs // OI)
    masked = (amplitudes * scale[None, :]).T

    sent = masked.reshape(OI, 32, OI, depth).transpose(1, 2, 0, 3)
    got = lax.all_to_all(sent, "row", split_axis=0, concat_axis=0, tiled=True)
    swapped = got.transpose(1, 0, 2, 3).reshape(pairs, depth)
    swapped, up4 = lax.optimization_barrier((swapped, up4))
    block = gather_four(place, integrals, up4, down4, far)

    both = jnp.stack([masked, swapped])
    pair = jnp.stack([both, chip_shift(both, (1, 0))])
    mine = [pair] + [chip_shift(pair, (0, dy)) for dy in (1, 3)]

    partner = x_swap(block)
    two = lax.ppermute(block, ("row", "col"), split_shift(2))
    mine.append(chip_shift(pair, (0, 2)))
    theirs = [core_swap(m) for m in mine]
    near = jnp.stack([block, partner])
    up = z_shift(near, 1)
    down = z_shift(near, -1)
    two_partner = x_swap(two)

    anywhere = pl.BlockSpec(memory_space=pl.ANY)
    scalars = pl.BlockSpec(memory_space=pltpu.SMEM)
    vector = pl.BlockSpec(memory_space=pltpu.VMEM)
    ints = pltpu.VMEM((2, 4, 2, rows, cols), jnp.bfloat16)
    params = pltpu.CompilerParams(vmem_limit_bytes=32 * 2**20)
    cost = pl.CostEstimate(
        flops=2 * pairs * 2048 * cols, bytes_accessed=10 * 2**20, transcendentals=0
    )
    total, kept = pl.pallas_call(
        first_half,
        out_shape=(
            jax.ShapeDtypeStruct((pairs, cols), jnp.float32),
            jax.ShapeDtypeStruct((2, 2, pairs, 8 * depth), jnp.bfloat16),
        ),
        in_specs=[scalars] + [anywhere] * 12,
        out_specs=(vector, vector),
        scratch_shapes=[ints, pltpu.SemaphoreType.DMA],
        compiler_params=params,
        cost_estimate=cost,
    )(place, *mine, *theirs, block, partner, two, two_partner)
    for shift, block, kind in ((1, down, jnp.float32), (-1, up, jnp.bfloat16)):
        total = pl.pallas_call(
            functools.partial(add_neighbour, shift),
            out_shape=jax.ShapeDtypeStruct((pairs, cols), kind),
            in_specs=[scalars, vector, vector, anywhere],
            out_specs=vector,
            scratch_shapes=[
                pltpu.VMEM((1, 4, 2, rows, cols), jnp.bfloat16),
                pltpu.SemaphoreType.DMA,
            ],
            compiler_params=params,
            cost_estimate=cost,
        )(place, total, kept, block)
    return total


def solution(mesh):
    in_specs = (P("col", "row"), P("row", "col"), P("col", "row"))
    out_specs = P("row", "col")
    return jax.shard_map(
        on_device, mesh=mesh, in_specs=in_specs, out_specs=out_specs, check_vma=False
    )
```

```python
import functools

import jax
import jax.numpy as jnp
from jax import lax
from jax.experimental import pallas as pl
from jax.experimental.pallas import tpu as pltpu
from jax.sharding import PartitionSpec as P

OI = 4
NTILE = 256


def z_shift(x, d):
    return lax.ppermute(x, "row", [(r, (r + 2 * d) % 32) for r in range(32)])


def split_shift(d):
    step = (2 * d, 32 - 2 * d)
    return [(r * 16 + c, (r + step[c % 2]) % 32 * 16 + c) for r in range(32) for c in range(16)]


def x_swap(x):
    return lax.ppermute(x, "row", [(r, r ^ 1) for r in range(32)])


def core_swap(x):
    return lax.ppermute(x, "col", [(c, c ^ 1) for c in range(16)])


def chip_shift(x, step):
    dx, dy = step
    return lax.ppermute(
        x, "col", [(c, (c // 8 ^ dx) * 8 + (c // 2 % 4 + dy) % 4 * 2 + c % 2) for c in range(16)]
    )


def multiply(amps, ints, cols):
    right = ints[:, :, :, :, cols].reshape(-1, NTILE)
    return jnp.dot(amps[0], right, preferred_element_type=jnp.float32) - jnp.dot(
        amps[1], right, preferred_element_type=jnp.float32
    )


def columns(n):
    return pl.ds(pl.multiple_of(n * NTILE, NTILE), NTILE)


def block_copies(place, refs, shifts, ints):
    z, xl = place[0], place[1]
    copies = []
    for ref, partner, shift in zip(refs[::2], refs[1::2], shifts):
        m = (z + shift) & 3
        copies.append((ref, ints.at[m >> 1, :, xl]))
        copies.append((partner, ints.at[m >> 1, :, 1 - xl]))
    return copies


def run_copies(copies, sem):
    copies = [pltpu.make_async_copy(a, b, sem) for a, b in copies]
    for copy in copies:
        copy.start()
    for copy in copies:
        copy.wait()


def four(place, here, below, above, far, out):
    q = place[0] >> 2
    for step, shard in enumerate((here, above, far, below)):
        out[(q + step) & 3] = shard[...]


def gather_four(place, *shards):
    return pl.pallas_call(
        four,
        out_shape=jax.ShapeDtypeStruct((4,) + shards[0].shape, shards[0].dtype),
        in_specs=[pl.BlockSpec(memory_space=pltpu.SMEM)]
        + [pl.BlockSpec(memory_space=pltpu.VMEM)] * 4,
        out_specs=pl.BlockSpec(memory_space=pltpu.VMEM),
    )(place, *shards)


def first_half(place, *refs):
    z, core, xh, y = place[0], place[2], place[3], place[4]
    mine, theirs, blocks = refs[:4], refs[4:8], refs[8:12]
    total, kept, ints, sem = refs[12:]
    copies = block_copies(place, blocks, (0, 2), ints)
    shards = []
    for refs, who in ((mine, core), (theirs, 1 - core)):
        for ref, dy in zip(refs, (0, 1, 3, 2)):
            for dx in range(2):
                shards.append((ref.at[dx], ((xh ^ dx) * 4 + ((y - dy) & 3)) * 2 + who))
    for ref, col in shards:
        slot = ((col >> 1) & 1) * 4 + (col >> 2)
        lanes = pl.ds(pl.multiple_of(slot * 128, 128), 128)
        for s in range(2):
            copies.append((ref.at[s], kept.at[(col + z) & 1, s, :, lanes]))
    run_copies(copies, sem)

    def tile(n, carry):
        cols = columns(n)
        total[:, cols] = multiply(kept.at[0], ints, cols)
        return carry

    lax.fori_loop(0, total.shape[1] // NTILE, tile, 0)


def add_neighbour(shift, place, total, kept, block, out, ints, sem):
    z, xl = place[0], place[1]
    run_copies([(block.at[0], ints.at[0, :, xl]), (block.at[1], ints.at[0, :, 1 - xl])], sem)
    depth = kept.shape[3] // 2
    lanes = pl.ds(pl.multiple_of((((z + shift) & 3) >> 1) * depth, depth), depth)

    def tile(n, carry):
        cols = columns(n)
        amps = [kept[1, s, :, lanes] for s in range(2)]
        out[:, cols] = (total[:, cols] + multiply(amps, ints, cols)).astype(out.dtype)
        return carry

    lax.fori_loop(0, out.shape[1] // NTILE, tile, 0)


def on_device(amplitudes, integrals, tile_mask):
    row, col = lax.axis_index("row"), lax.axis_index("col")
    core = col % 2
    place = jnp.stack([row // 2, row % 2, core, col // 8, col // 2 % 4]).astype(jnp.int32)
    rows, cols = integrals.shape
    depth, pairs = amplitudes.shape

    up4 = z_shift(integrals, 4)
    down4 = z_shift(integrals, -4)
    far = lax.ppermute(jnp.where(core == 0, up4, down4), ("row", "col"), split_shift(4))

    scale = jnp.repeat(tile_mask.astype(jnp.bfloat16).reshape(-1), pairs // OI)
    masked = (amplitudes * scale[None, :]).T

    sent = masked.reshape(OI, 32, OI, depth).transpose(1, 2, 0, 3)
    got = lax.all_to_all(sent, "row", split_axis=0, concat_axis=0, tiled=True)
    swapped = got.transpose(1, 0, 2, 3).reshape(pairs, depth)
    swapped, up4, down4 = lax.optimization_barrier((swapped, up4, down4))
    block = gather_four(place, integrals, up4, down4, far)

    both = jnp.stack([masked, swapped])
    pair = jnp.stack([both, chip_shift(both, (1, 0))])
    mine = [pair] + [chip_shift(pair, (0, dy)) for dy in (1, 3)]

    partner = x_swap(block)
    two = lax.ppermute(block, ("row", "col"), split_shift(2))
    mine.append(chip_shift(pair, (0, 2)))
    theirs = [core_swap(m) for m in mine]
    near = jnp.stack([block, partner])
    up = z_shift(near, 1)
    down = z_shift(near, -1)
    two_partner = x_swap(two)

    anywhere = pl.BlockSpec(memory_space=pl.ANY)
    scalars = pl.BlockSpec(memory_space=pltpu.SMEM)
    vector = pl.BlockSpec(memory_space=pltpu.VMEM)
    ints = pltpu.VMEM((2, 4, 2, rows, cols), jnp.bfloat16)
    params = pltpu.CompilerParams(vmem_limit_bytes=32 * 2**20)
    cost = pl.CostEstimate(
        flops=2 * pairs * 2048 * cols, bytes_accessed=10 * 2**20, transcendentals=0
    )
    total, kept = pl.pallas_call(
        first_half,
        out_shape=(
            jax.ShapeDtypeStruct((pairs, cols), jnp.float32),
            jax.ShapeDtypeStruct((2, 2, pairs, 8 * depth), jnp.bfloat16),
        ),
        in_specs=[scalars] + [anywhere] * 12,
        out_specs=(vector, vector),
        scratch_shapes=[ints, pltpu.SemaphoreType.DMA],
        compiler_params=params,
        cost_estimate=cost,
    )(place, *mine, *theirs, block, partner, two, two_partner)
    for shift, block, kind in ((1, down, jnp.float32), (-1, up, jnp.bfloat16)):
        total = pl.pallas_call(
            functools.partial(add_neighbour, shift),
            out_shape=jax.ShapeDtypeStruct((pairs, cols), kind),
            in_specs=[scalars, vector, vector, anywhere],
            out_specs=vector,
            scratch_shapes=[
                pltpu.VMEM((1, 4, 2, rows, cols), jnp.bfloat16),
                pltpu.SemaphoreType.DMA,
            ],
            compiler_params=params,
            cost_estimate=cost,
        )(place, total, kept, block)
    return total


def solution(mesh):
    in_specs = (P("col", "row"), P("row", "col"), P("col", "row"))
    out_specs = P("row", "col")
    return jax.shard_map(
        on_device, mesh=mesh, in_specs=in_specs, out_specs=out_specs, check_vma=False
    )
```

```python
import functools

import jax
import jax.numpy as jnp
from jax import lax
from jax.experimental import pallas as pl
from jax.experimental.pallas import tpu as pltpu
from jax.sharding import PartitionSpec as P

OI = 4
NTILE = 512


def z_shift(x, d):
    return lax.ppermute(x, "row", [(r, (r + 2 * d) % 32) for r in range(32)])


def split_shift(d):
    step = (2 * d, 32 - 2 * d)
    return [(r * 16 + c, (r + step[c % 2]) % 32 * 16 + c) for r in range(32) for c in range(16)]


def x_swap(x):
    return lax.ppermute(x, "row", [(r, r ^ 1) for r in range(32)])


def core_swap(x):
    return lax.ppermute(x, "col", [(c, c ^ 1) for c in range(16)])


def chip_shift(x, step):
    dx, dy = step
    return lax.ppermute(
        x, "col", [(c, (c // 8 ^ dx) * 8 + (c // 2 % 4 + dy) % 4 * 2 + c % 2) for c in range(16)]
    )


def multiply(amps, ints, cols):
    right = ints[:, :, :, :, cols].reshape(-1, NTILE)
    return jnp.dot(amps[0], right, preferred_element_type=jnp.float32) - jnp.dot(
        amps[1], right, preferred_element_type=jnp.float32
    )


def columns(n):
    return pl.ds(pl.multiple_of(n * NTILE, NTILE), NTILE)


def block_copies(place, refs, shifts, ints):
    z, xl = place[0], place[1]
    copies = []
    for ref, partner, shift in zip(refs[::2], refs[1::2], shifts):
        m = (z + shift) & 3
        copies.append((ref, ints.at[m >> 1, :, xl]))
        copies.append((partner, ints.at[m >> 1, :, 1 - xl]))
    return copies


def run_copies(copies, sem):
    copies = [pltpu.make_async_copy(a, b, sem) for a, b in copies]
    for copy in copies:
        copy.start()
    for copy in copies:
        copy.wait()


def four(place, here, below, above, far, out):
    q = place[0] >> 2
    for step, shard in enumerate((here, above, far, below)):
        out[(q + step) & 3] = shard[...]


def gather_four(place, *shards):
    return pl.pallas_call(
        four,
        out_shape=jax.ShapeDtypeStruct((4,) + shards[0].shape, shards[0].dtype),
        in_specs=[pl.BlockSpec(memory_space=pltpu.SMEM)]
        + [pl.BlockSpec(memory_space=pltpu.VMEM)] * 4,
        out_specs=pl.BlockSpec(memory_space=pltpu.VMEM),
    )(place, *shards)


def first_half(place, *refs):
    z, core, xh, y = place[0], place[2], place[3], place[4]
    mine, theirs, blocks = refs[:4], refs[4:8], refs[8:12]
    total, kept, ints, sem = refs[12:]
    copies = block_copies(place, blocks, (0, 2), ints)
    shards = []
    for refs, who in ((mine, core), (theirs, 1 - core)):
        for ref, dy in zip(refs, (0, 1, 3, 2)):
            for dx in range(2):
                shards.append((ref.at[dx], ((xh ^ dx) * 4 + ((y - dy) & 3)) * 2 + who))
    for ref, col in shards:
        slot = ((col >> 1) & 1) * 4 + (col >> 2)
        lanes = pl.ds(pl.multiple_of(slot * 128, 128), 128)
        for s in range(2):
            copies.append((ref.at[s], kept.at[(col + z) & 1, s, :, lanes]))
    run_copies(copies, sem)

    def tile(n, carry):
        cols = columns(n)
        total[:, cols] = multiply(kept.at[0], ints, cols)
        return carry

    lax.fori_loop(0, total.shape[1] // NTILE, tile, 0)


def add_neighbour(shift, place, total, kept, block, out, ints, sem):
    z, xl = place[0], place[1]
    run_copies([(block.at[0], ints.at[0, :, xl]), (block.at[1], ints.at[0, :, 1 - xl])], sem)
    depth = kept.shape[3] // 2
    lanes = pl.ds(pl.multiple_of((((z + shift) & 3) >> 1) * depth, depth), depth)

    def tile(n, carry):
        cols = columns(n)
        amps = [kept[1, s, :, lanes] for s in range(2)]
        out[:, cols] = (total[:, cols] + multiply(amps, ints, cols)).astype(out.dtype)
        return carry

    lax.fori_loop(0, out.shape[1] // NTILE, tile, 0)


def on_device(amplitudes, integrals, tile_mask):
    row, col = lax.axis_index("row"), lax.axis_index("col")
    core = col % 2
    place = jnp.stack([row // 2, row % 2, core, col // 8, col // 2 % 4]).astype(jnp.int32)
    rows, cols = integrals.shape
    depth, pairs = amplitudes.shape

    up4 = z_shift(integrals, 4)
    down4 = z_shift(integrals, -4)
    far = lax.ppermute(jnp.where(core == 0, up4, down4), ("row", "col"), split_shift(4))

    scale = jnp.repeat(tile_mask.astype(jnp.bfloat16).reshape(-1), pairs // OI)
    masked = (amplitudes * scale[None, :]).T

    sent = masked.reshape(OI, 32, OI, depth).transpose(1, 2, 0, 3)
    got = lax.all_to_all(sent, "row", split_axis=0, concat_axis=0, tiled=True)
    swapped = got.transpose(1, 0, 2, 3).reshape(pairs, depth)
    swapped, up4, down4 = lax.optimization_barrier((swapped, up4, down4))
    block = gather_four(place, integrals, up4, down4, far)

    both = jnp.stack([masked, swapped])
    pair = jnp.stack([both, chip_shift(both, (1, 0))])
    mine = [pair] + [chip_shift(pair, (0, dy)) for dy in (1, 3)]

    partner = x_swap(block)
    two = lax.ppermute(block, ("row", "col"), split_shift(2))
    mine.append(chip_shift(pair, (0, 2)))
    theirs = [core_swap(m) for m in mine]
    near = jnp.stack([block, partner])
    up = z_shift(near, 1)
    down = z_shift(near, -1)
    two_partner = x_swap(two)

    anywhere = pl.BlockSpec(memory_space=pl.ANY)
    scalars = pl.BlockSpec(memory_space=pltpu.SMEM)
    vector = pl.BlockSpec(memory_space=pltpu.VMEM)
    ints = pltpu.VMEM((2, 4, 2, rows, cols), jnp.bfloat16)
    params = pltpu.CompilerParams(vmem_limit_bytes=32 * 2**20)
    cost = pl.CostEstimate(
        flops=2 * pairs * 2048 * cols, bytes_accessed=10 * 2**20, transcendentals=0
    )
    total, kept = pl.pallas_call(
        first_half,
        out_shape=(
            jax.ShapeDtypeStruct((pairs, cols), jnp.float32),
            jax.ShapeDtypeStruct((2, 2, pairs, 8 * depth), jnp.bfloat16),
        ),
        in_specs=[scalars] + [anywhere] * 12,
        out_specs=(vector, vector),
        scratch_shapes=[ints, pltpu.SemaphoreType.DMA],
        compiler_params=params,
        cost_estimate=cost,
    )(place, *mine, *theirs, block, partner, two, two_partner)
    for shift, block, kind in ((1, down, jnp.float32), (-1, up, jnp.bfloat16)):
        total = pl.pallas_call(
            functools.partial(add_neighbour, shift),
            out_shape=jax.ShapeDtypeStruct((pairs, cols), kind),
            in_specs=[scalars, vector, vector, anywhere],
            out_specs=vector,
            scratch_shapes=[
                pltpu.VMEM((1, 4, 2, rows, cols), jnp.bfloat16),
                pltpu.SemaphoreType.DMA,
            ],
            compiler_params=params,
            cost_estimate=cost,
        )(place, total, kept, block)
    return total


def solution(mesh):
    in_specs = (P("col", "row"), P("row", "col"), P("col", "row"))
    out_specs = P("row", "col")
    return jax.shard_map(
        on_device, mesh=mesh, in_specs=in_specs, out_specs=out_specs, check_vma=False
    )
```
